32 devices in a mesh: dp: 8 (over y, x, core), mp: 4 (over z).
Axes of the slice: x: 2, y: 2, z: 4, core: 2. Of those that a mesh axis runs over, the one named last changes fastest.
Arguments:
- tokens: bfloat16 [16384, 1024], P(('dp', 'mp')), may hold values from -6 to 6
- memory: bfloat16 [16384, 1024], P(('dp', 'mp')), may hold values from -6 to 6
- mem_lengths: int32 [16], P('dp'), may hold values from 256 to 1024, as said below
- cotangent: bfloat16 [16384, 1024], P(('dp', 'mp')), may hold values from -7.5 to 7.5
- attn_weights: float32 [8, 1024, 1024], P(None, 'dp', 'mp'), may hold values from -0.5 to 0.5
- ffn_weights: float32 [2, 1024, 4096], P(None, 'dp', 'mp'), may hold values from -0.25 to 0.25
- attn_momentum: float32 [8, 1024, 1024], P(None, 'dp', 'mp'), may hold values from -96 to 96
- ffn_momentum: float32 [2, 1024, 4096], P(None, 'dp', 'mp'), may hold values from -192 to 192
- norm_params: float32 [2, 3, 1024], replicated, may hold values from -0.8 to 1.3
- norm_first: float32 [2, 3, 1024], replicated, may hold values from -80 to 80
- norm_second: float32 [2, 3, 1024], replicated, may hold values from 16.384 to 65.536
Outputs:
- mixed_out: float32 [16384, 1024], P(('dp', 'mp'))
- input_grad: float32 [16384, 1024], P(('dp', 'mp'))
- memory_grad: float32 [16384, 1024], P(('dp', 'mp'))
- attn_weights_new: float32 [8, 1024, 1024], P(None, 'dp', 'mp')
- attn_momentum_new: float32 [8, 1024, 1024], P(None, 'dp', 'mp')
- ffn_weights_new: float32 [2, 1024, 4096], P(None, 'dp', 'mp')
- ffn_momentum_new: float32 [2, 1024, 4096], P(None, 'dp', 'mp')
- norm_grad_sums: float32 [2, 3, 1024], replicated
- norm_params_new: float32 [2, 3, 1024], replicated
- norm_first_new: float32 [2, 3, 1024], replicated
- norm_second_new: float32 [2, 3, 1024], replicated
The draws below stay inside these ranges and needn't reach their ends.
Inputs may be any that keep to these rules, and one draw needn't show every extreme that they name: `mem_lengths`: each sequence's memory is valid at its first positions; one sequence has all 1024, one has 256.
All inputs are finite; a program needn't handle non-finite values.
Results may differ from the reference program's by a relative error of at most 0.015.
Values may be sent and summed in bfloat16 or wider, within the bound.
No kernel may reach another device: no remote copies, remote signals or barrier semaphores. Data moves between devices by JAX's collectives and lax.ppermute only.
A program may use at most 256 MiB of HBM per device.

```python
import math
import jax
import jax.numpy as jnp
from jax import lax

D = 1024
H = 16
HD = 64
FF = 4096
L = 1024
MEM = 1024
SEQ_DP = 2
MB = 128
NS = 5
SEQUENCES = 16
TOKENS = 16384
MTOKENS = 16384
N_DP = 8


def draw_mem_lengths(key, part):
    key_len, key_pick = jax.random.split(key)
    drawn = jax.random.randint(key_len, (SEQUENCES,), MEM // 4, MEM + 1)
    chosen = jax.random.randint(key_pick, (), 0, SEQUENCES)
    places = jnp.arange(SEQUENCES)
    shortest = jnp.where(places == (chosen + 1) % SEQUENCES, MEM // 4, drawn)
    return jnp.where(places == chosen, MEM, shortest).astype(jnp.int32)


def draw_cotangent(key, part):
    key_rows = jax.random.fold_in(key, 0)
    position = jnp.arange(TOKENS, dtype=jnp.float32)[:, None] / TOKENS
    ramp = 0.5 + position
    return (jnp.clip(jax.random.normal(key_rows, (TOKENS, D), jnp.float32), -5.0, 5.0) * ramp).astype(jnp.bfloat16)


def draw_attn_weights(key, part):
    slot_scale = jnp.array([1.0, 1.0, 1.0, 4.0, 1.0, 1.0, 1.0, 4.0], jnp.float32) * D ** (-0.5)
    base = jnp.clip(jax.random.normal(key, (8, D, D), jnp.float32), -4.0, 4.0)
    return base * slot_scale[:, None, None]


def draw_ffn_weights(key, part):
    slot_scale = jnp.array([D ** (-0.5), 4.0 * FF ** (-0.5)], jnp.float32)
    base = jnp.clip(jax.random.normal(key, (2, D, FF), jnp.float32), -4.0, 4.0)
    return base * slot_scale[:, None, None]


def draw_norm_params(key, part):
    key_gain, key_bias = jax.random.split(key)
    gains = 1.0 + jax.random.uniform(key_gain, (1, 3, D), jnp.float32, -0.3, 0.3)
    biases = jnp.clip(0.2 * jax.random.normal(key_bias, (1, 3, D), jnp.float32), -0.8, 0.8)
    return jnp.concatenate([gains, biases], axis=0)


def level_of(own_key, shape, pieces, smallest, high):
    factor_of, own = 1.0, jax.random.fold_in(own_key, 6)
    for axis_at, parts in pieces:
        steps = jnp.exp(jax.random.uniform(jax.random.fold_in(own, axis_at), (parts,), jnp.float32, smallest / len(pieces), high / len(pieces)))
        factor_of = factor_of * jnp.repeat(steps, shape[axis_at] // parts).reshape([-1 if axis == axis_at else 1 for axis in range(len(shape))])
    return factor_of


def scatter_about(rng, shape, width, reach, shards=(), kind=jnp.bfloat16):
    loudness = level_of(rng, shape, shards, -0.22, 0.18) if shards else 1.0
    values = jax.random.normal(rng, shape, jnp.float32) * width * loudness
    return jnp.minimum(jnp.maximum(values, -reach), reach).astype(kind)


def setup_inputs(seed: int = 0) -> dict:
    arg_keys = jax.random.split(jax.random.key(seed), 12)
    return {
        "tokens": scatter_about(arg_keys[0], (TOKENS, D), 1.0, 6.0, ((0, 32),)),
        "memory": scatter_about(arg_keys[1], (MTOKENS, D), 1.0, 6.0, ((0, 32),)),
        "mem_lengths": draw_mem_lengths(jax.random.fold_in(arg_keys[11], 71), 0),
        "cotangent": draw_cotangent(jax.random.fold_in(arg_keys[11], 71), 0),
        "attn_weights": draw_attn_weights(jax.random.fold_in(arg_keys[11], 71), 0),
        "ffn_weights": draw_ffn_weights(jax.random.fold_in(arg_keys[11], 71), 0),
        "attn_momentum": scatter_about(arg_keys[6], (8, D, D), (TOKENS ** 0.5 / 8), 96.0, ((1, 8), (2, 4)), jnp.float32),
        "ffn_momentum": scatter_about(arg_keys[7], (2, D, FF), (TOKENS ** 0.5 / 4), 192.0, ((1, 8), (2, 4)), jnp.float32),
        "norm_params": draw_norm_params(jax.random.fold_in(arg_keys[11], 71), 0),
        "norm_first": scatter_about(arg_keys[9], (2, 3, D), (0.11 * TOKENS ** 0.5), 80.0, (), jnp.float32),
        "norm_second": jnp.clip(jnp.exp(jax.random.uniform(arg_keys[10], (2, 3, D), jnp.float32, math.log(16.384), math.log(65.536))), 16.384, 65.536),
    }


@jax.custom_vjp
def low(v):
    return lax.optimization_barrier(v.astype(jnp.bfloat16)).astype(jnp.float32)

@jax.custom_vjp
def low_back(v):
    return v

def low_keep(v):
    return (low(v), None)

def low_pass(kept, grad):
    return (grad,)

def back_keep(v):
    return (v, None)

def back_low(kept, grad):
    return (low(grad),)
low.defvjp(low_keep, low_pass)
low_back.defvjp(back_keep, back_low)
highest = lax.Precision.HIGHEST
res_scale = 300.0 ** 0.25
coef_one = 3.4445
coef_two = -4.775
coef_three = 2.0315
muon_rate = 0.3
adam_rate = 0.2
adam_count = 10.0

def matmul(left, right):
    return jnp.dot(left, right, precision=highest, preferred_element_type=jnp.float32)

def gelu_exact(value):
    return 0.5 * value * (1.0 + lax.erf(value * 2.0 ** (-0.5)))

def layer_norm(resid, gain, bias):
    row_mean = lax.optimization_barrier(jnp.mean(resid, axis=-1, keepdims=True))
    centred = resid - row_mean
    variance = lax.optimization_barrier(jnp.mean(centred * centred, axis=-1, keepdims=True))
    return centred * lax.rsqrt(variance + 1e-05) * gain + bias

def attend(query_rows, key_rows, value_rows, allowed):
    score_scale = HD ** (-0.5)
    scores = low_back(score_scale * jnp.einsum('qhd,khd->hqk', query_rows, key_rows, precision=highest))
    masked = jnp.where(allowed, scores, -1e+30)
    row_max = lax.optimization_barrier(jnp.max(masked, axis=-1, keepdims=True))
    lifted = jnp.exp(masked - row_max)
    attn_probs = lifted / lax.optimization_barrier(jnp.sum(lifted, axis=-1, keepdims=True))
    return jnp.einsum('hqk,khd->qhd', low(attn_probs), value_rows, precision=highest)

def forward(token_rows, memory_rows, lengths, attn_w, ffn_w, norm_p):
    seq_count = lengths.shape[0]
    attn_low = low(attn_w)
    ffn_low = low(ffn_w)

    def heads(rows):
        return rows.reshape(seq_count, -1, H, HD)

    def project(rows, weight):
        return low(low_back(matmul(rows, weight)))
    causal = jnp.arange(L)[:, None] >= jnp.arange(L)[None, :]

    def self_block(inputs):
        return attend(inputs[0], inputs[1], inputs[2], causal[None])

    def cross_block(inputs):
        allowed = jnp.arange(MEM)[None, None, :] < inputs[3]
        return attend(inputs[0], inputs[1], inputs[2], allowed)
    self_q = heads(project(token_rows, attn_low[0]))
    self_k = heads(project(token_rows, attn_low[1]))
    self_v = heads(project(token_rows, attn_low[2]))
    self_ctx = lax.map(jax.checkpoint(self_block), (self_q, self_k, self_v))
    self_ctx = low(low_back(self_ctx.reshape(-1, D)))
    self_out = low_back(matmul(self_ctx, attn_low[3].T))
    first_out = layer_norm(res_scale * token_rows + self_out, norm_p[0, 0], norm_p[1, 0])
    first_low = low(first_out)
    cross_q = heads(project(first_low, attn_low[4]))
    cross_k = heads(project(memory_rows, attn_low[5]))
    cross_v = heads(project(memory_rows, attn_low[6]))
    cross_ctx = lax.map(jax.checkpoint(cross_block), (cross_q, cross_k, cross_v, lengths))
    cross_ctx = low(low_back(cross_ctx.reshape(-1, D)))
    cross_out = low_back(matmul(cross_ctx, attn_low[7].T))
    second = layer_norm(res_scale * first_out + cross_out, norm_p[0, 1], norm_p[1, 1])
    hidden = matmul(low(second), ffn_low[0])
    active = low(low_back(gelu_exact(hidden)))
    ffn_out = low_back(matmul(active, ffn_low[1].T))
    return layer_norm(res_scale * second + ffn_out, norm_p[0, 2], norm_p[1, 2])

def orthogonal(moment):
    slots, rows, cols = moment.shape
    blocks = moment.reshape(slots, rows, cols // MB, MB)
    norms = jnp.sqrt(lax.optimization_barrier(jnp.sum(blocks * blocks, axis=(1, 3), keepdims=True)))
    current = blocks / (norms + 1e-07)
    for sweep_index in range(NS):
        gram = jnp.einsum('sdbi,sdbj->sbij', current, current, precision=highest)
        squared = jnp.einsum('sbij,sbjk->sbik', gram, gram, precision=highest)
        poly = coef_two * gram + coef_three * squared
        current = coef_one * current + jnp.einsum('sdbi,sbij->sdbj', current, poly, precision=highest)
    return current.reshape(slots, rows, cols)

def reference(tokens, memory, mem_lengths, cotangent, attn_weights, ffn_weights, attn_momentum, ffn_momentum, norm_params, norm_first, norm_second):
    group_rows = SEQ_DP * L
    token_groups = tokens.astype(jnp.float32).reshape(N_DP, group_rows, D)
    memory_groups = memory.astype(jnp.float32).reshape(N_DP, SEQ_DP * MEM, D)
    length_groups = mem_lengths.reshape(N_DP, SEQ_DP)
    upstream_groups = cotangent.astype(jnp.float32).reshape(N_DP, group_rows, D)

    def group_step(carry, inputs):
        token_rows, memory_rows, lengths, upstream = inputs

        def local(rows, mem_rows, attn_w, ffn_w, norm_p):
            return forward(rows, mem_rows, lengths, attn_w, ffn_w, norm_p)
        mixed_rows, pullback = jax.vjp(local, token_rows, memory_rows, attn_weights, ffn_weights, norm_params)
        grad_rows, grad_memory, grad_attn, grad_ffn, grad_norm = pullback(upstream)
        carry = (carry[0] + grad_attn, carry[1] + grad_ffn, carry[2] + grad_norm)
        return (carry, (mixed_rows, grad_rows, grad_memory))
    start = (jnp.zeros_like(attn_weights), jnp.zeros_like(ffn_weights), jnp.zeros_like(norm_params))
    totals, outputs = lax.scan(group_step, start, (token_groups, memory_groups, length_groups, upstream_groups))
    grad_attn, grad_ffn, grad_norm = totals
    mixed_out = outputs[0].reshape(TOKENS, D)
    input_grad = outputs[1].reshape(TOKENS, D)
    memory_grad = outputs[2].reshape(MTOKENS, D)
    attn_momentum_new = 0.5 * attn_momentum + grad_attn
    ffn_momentum_new = 0.5 * ffn_momentum + grad_ffn
    step_scale = muon_rate * (D / MB) ** 0.5
    attn_weights_new = attn_weights - step_scale * orthogonal(attn_momentum_new)
    ffn_weights_new = ffn_weights - step_scale * orthogonal(ffn_momentum_new)
    norm_first_new = 0.9 * norm_first + 0.1 * grad_norm
    norm_second_new = 0.999 * norm_second + 0.001 * grad_norm * grad_norm
    step_size = norm_first_new / (1.0 - 0.9 ** adam_count) / (jnp.sqrt(norm_second_new / (1.0 - 0.999 ** adam_count)) + 1e-08)
    norm_params_new = norm_params - adam_rate * step_size
    return (mixed_out, input_grad, memory_grad, attn_weights_new, attn_momentum_new, ffn_weights_new, ffn_momentum_new, grad_norm, norm_params_new, norm_first_new, norm_second_new)
```

```python
import functools

import jax
import jax.numpy as jnp
from jax import lax
from jax.experimental import pallas as pl
from jax.experimental.pallas import tpu as pltpu
from jax.sharding import Mesh, PartitionSpec as P

HD = 64
MB = 128
NS = 5
PAIR = 2 * HD
QCHUNK = 256
highest = lax.Precision.HIGHEST
res_scale = 300.0**0.25
coef_one = 3.4445
coef_two = -4.775
coef_three = 2.0315
muon_rate = 0.3
adam_rate = 0.2
adam_count = 10.0
score_scale = HD ** (-0.5)
f32 = jnp.float32
bf16 = jnp.bfloat16


def gelu_exact(value):
    return 0.5 * value * (1.0 + lax.erf(value * 2.0 ** (-0.5)))


def gelu_slope(value):
    return 0.5 * (1.0 + lax.erf(value * 2.0 ** (-0.5))) + value * jnp.exp(-0.5 * value * value) * (
        2.0 * 3.141592653589793
    ) ** (-0.5)


def norm_forward(resid, gain, bias):
    row_mean = jnp.mean(resid, axis=-1, keepdims=True)
    centred = resid - row_mean
    variance = jnp.mean(centred * centred, axis=-1, keepdims=True)
    inv_std = lax.rsqrt(variance + 1e-05)
    normed = centred * inv_std
    return (normed * gain + bias, normed, inv_std)


def norm_backward(upstream, normed, inv_std, gain):
    scaled = upstream * gain
    centred = scaled - jnp.mean(scaled, axis=-1, keepdims=True)
    grad_resid = inv_std * (centred - normed * jnp.mean(scaled * normed, axis=-1, keepdims=True))
    return (grad_resid, jnp.sum(upstream * normed, axis=0), jnp.sum(upstream, axis=0))


def nt_dot(left, right):
    return lax.dot_general(left, right, (((1,), (1,)), ((), ())), preferred_element_type=f32)


def nn_dot(left, right):
    return lax.dot_general(left, right, (((1,), (0,)), ((), ())), preferred_element_type=f32)


def flip(value):
    return jnp.transpose(value).astype(bf16)


def only_head(value, head):
    lane = lax.broadcasted_iota(jnp.int32, value.shape, 1)
    keep = (lane < HD) if head == 0 else (lane >= HD)
    return jnp.where(keep, value, 0.0).astype(bf16)


def in_place_order(ref, slot, shift):
    half = ref.shape[-2] // 2
    low = ref[slot, pl.ds(pl.multiple_of(shift, half), half), :]
    high = ref[slot, pl.ds(pl.multiple_of(half - shift, half), half), :]
    return jnp.concatenate([low.astype(f32), high.astype(f32)], axis=0)


def row_of(start, shift, count, chunk, causal):
    if not causal:
        return pl.ds(start, chunk)
    row = start + shift
    row = jnp.where(row >= count, row - count, row)
    return pl.ds(pl.multiple_of(row, chunk), chunk)


def key_span(causal, start, size, key_count):
    return min(start + size, key_count) if causal else key_count


def scores_by_key(keys, queries, start, length, causal):
    scores = nt_dot(keys, queries)
    key_at = lax.broadcasted_iota(jnp.int32, scores.shape, 0)
    if causal:
        query_at = start + lax.broadcasted_iota(jnp.int32, scores.shape, 1)
        return jnp.where(key_at <= query_at, scores, -1e30)
    return jnp.where(key_at < length, scores, -1e30)


def forward_kernel(causal, chunk, at_ref, q_ref, k_ref, v_ref, ctx_ref, lse_ref):
    queries, key_count = q_ref.shape[-2], k_ref.shape[-2]
    length, shift = at_ref[0], at_ref[1]
    keys = in_place_order(k_ref, 0, shift) * score_scale
    values_t = flip(in_place_order(v_ref, 0, shift))
    scaled = [only_head(keys, head) for head in (0, 1)]
    for start in range(0, queries, chunk):
        span = key_span(causal, start, chunk, key_count)
        rows = row_of(start, shift, queries, chunk, causal)
        query_rows = q_ref[0, rows, :]
        parts = []
        for head in (0, 1):
            scores = scores_by_key(scaled[head][:span], query_rows, start, length, causal)
            top = jnp.max(scores, axis=0, keepdims=True)
            lifted = jnp.exp(scores - top)
            total = jnp.sum(lifted, axis=0, keepdims=True)
            mixed = nn_dot(values_t[head * HD : (head + 1) * HD, :span], lifted.astype(bf16))
            parts.append(mixed / total)
            lse_ref[0, head : head + 1, start : start + chunk] = top + jnp.log(total)
        both = jnp.concatenate(parts, axis=0)
        ctx_ref[rows, :] = jnp.transpose(both).astype(bf16)


def backward_kernel(
    causal, chunk, at_ref, q_ref, k_ref, v_ref, ctx_ref, grad_ref, lse_ref,
    gq_ref, gkv_ref, gk_acc, gv_acc,
):
    queries, key_count = q_ref.shape[-2], k_ref.shape[-2]
    length, shift = at_ref[0], at_ref[1]
    keys = in_place_order(k_ref, 0, shift) * score_scale
    values = in_place_order(v_ref, 0, shift)
    scaled = [only_head(keys, head) for head in (0, 1)]
    lane_values = [only_head(values, head) for head in (0, 1)]
    scaled_t = flip(keys)
    gk_acc[...] = jnp.zeros_like(gk_acc)
    gv_acc[...] = jnp.zeros_like(gv_acc)
    for start in range(0, queries, chunk):
        span = key_span(causal, start, chunk, key_count)
        rows = row_of(start, shift, queries, chunk, causal)
        query_rows = q_ref[0, rows, :]
        grad_rows = grad_ref[rows, :]
        query_wide, grad_wide = query_rows.astype(f32), grad_rows.astype(f32)
        inner = jnp.transpose(grad_wide * ctx_ref[rows, :].astype(f32))
        parts = []
        for head in (0, 1):
            scores = scores_by_key(scaled[head][:span], query_rows, start, length, causal)
            probs = jnp.exp(scores - lse_ref[0, head : head + 1, start : start + chunk])
            grad_probs = nt_dot(lane_values[head][:span], grad_rows)
            delta = jnp.sum(inner[head * HD : (head + 1) * HD], axis=0, keepdims=True)
            grad_scores = (probs * (grad_probs - delta)).astype(bf16)
            gv_acc[:span, :] += nn_dot(probs.astype(bf16), only_head(grad_wide, head))
            gk_acc[:span, :] += nn_dot(grad_scores, only_head(query_wide, head))
            parts.append(nn_dot(scaled_t[head * HD : (head + 1) * HD, :span], grad_scores))
        gq_ref[rows, :] = jnp.transpose(jnp.concatenate(parts, axis=0)).astype(bf16)
    half = key_count // 2
    low = pl.ds(pl.multiple_of(shift, half), half)
    high = pl.ds(pl.multiple_of(half - shift, half), half)
    gkv_ref[0, low, :] = (gk_acc[:half, :] * score_scale).astype(bf16)
    gkv_ref[0, high, :] = (gk_acc[half:, :] * score_scale).astype(bf16)
    gkv_ref[1, low, :] = gv_acc[:half, :].astype(bf16)
    gkv_ref[1, high, :] = gv_acc[half:, :].astype(bf16)


def source_block(rows, slot):
    return pl.BlockSpec((1, rows, PAIR), lambda pair, at: (slot, 0, pair))


def attend_forward(query_src, key_src, value_src, at, causal):
    queries, cols = query_src[0].shape[1:]
    key_count = key_src[0].shape[1]
    chunk = min(QCHUNK, queries // 2)
    work = queries * key_count * cols
    return pl.pallas_call(
        functools.partial(forward_kernel, causal, chunk),
        grid_spec=pltpu.PrefetchScalarGridSpec(
            num_scalar_prefetch=1,
            grid=(cols // PAIR,),
            in_specs=[
                source_block(queries, query_src[1]),
                source_block(key_count, key_src[1]),
                source_block(key_count, value_src[1]),
            ],
            out_specs=[
                pl.BlockSpec((queries, PAIR), lambda pair, at: (0, pair)),
                pl.BlockSpec((1, 8, queries), lambda pair, at: (pair, 0, 0)),
            ],
        ),
        out_shape=[
            jax.ShapeDtypeStruct((queries, cols), bf16),
            jax.ShapeDtypeStruct((cols // PAIR, 8, queries), f32),
        ],
        compiler_params=pltpu.CompilerParams(vmem_limit_bytes=48 * 2**20),
        cost_estimate=pl.CostEstimate(
            flops=32 * work, bytes_accessed=8 * queries * cols, transcendentals=work // HD
        ),
        name="attend_forward_causal" if causal else "attend_forward_cross",
    )(at, query_src[0], key_src[0], value_src[0])


def attend_backward(query_src, key_src, value_src, at, ctx, grad_ctx, lse, causal):
    queries, cols = query_src[0].shape[1:]
    key_count = key_src[0].shape[1]
    chunk = min(QCHUNK, queries // 2)
    flat = pl.BlockSpec((queries, PAIR), lambda pair, at: (0, pair))
    work = queries * key_count * cols
    return pl.pallas_call(
        functools.partial(backward_kernel, causal, chunk),
        grid_spec=pltpu.PrefetchScalarGridSpec(
            num_scalar_prefetch=1,
            grid=(cols // PAIR,),
            in_specs=[
                source_block(queries, query_src[1]),
                source_block(key_count, key_src[1]),
                source_block(key_count, value_src[1]),
                flat,
                flat,
                pl.BlockSpec((1, 8, queries), lambda pair, at: (pair, 0, 0)),
            ],
            out_specs=[flat, pl.BlockSpec((2, key_count, PAIR), lambda pair, at: (0, 0, pair))],
            scratch_shapes=[pltpu.VMEM((key_count, PAIR), f32), pltpu.VMEM((key_count, PAIR), f32)],
        ),
        out_shape=[
            jax.ShapeDtypeStruct((queries, cols), bf16),
            jax.ShapeDtypeStruct((2, key_count, cols), bf16),
        ],
        compiler_params=pltpu.CompilerParams(vmem_limit_bytes=48 * 2**20),
        cost_estimate=pl.CostEstimate(
            flops=40 * work, bytes_accessed=16 * queries * cols, transcendentals=work // HD
        ),
        name="attend_backward_causal" if causal else "attend_backward_cross",
    )(at, query_src[0], key_src[0], value_src[0], ctx, grad_ctx, lse)


def assemble_kernel(at_ref, own_ref, inner_ref, outer_ref, far_low_ref, far_high_ref, out_ref):
    which = pl.program_id(1) ^ at_ref[0]
    half = far_low_ref.shape[1]

    for code, ref in ((0, own_ref), (1, inner_ref), (2, outer_ref)):
        @pl.when(which == code)
        def _(ref=ref):
            out_ref[...] = ref[...]

    @pl.when(which == 3)
    def _():
        out_ref[:, :half, :] = far_low_ref[...]
        out_ref[:, half:, :] = far_high_ref[...]


def assemble(position, own, inner, outer, far_low, far_high):
    slots, rows, cols = own.shape
    whole = pl.BlockSpec((1, rows, cols), lambda slot, block, at: (slot, 0, 0))
    half = pl.BlockSpec((1, rows // 2, cols), lambda slot, block, at: (slot, 0, 0))
    return pl.pallas_call(
        assemble_kernel,
        grid_spec=pltpu.PrefetchScalarGridSpec(
            num_scalar_prefetch=1,
            grid=(slots, 4),
            in_specs=[whole, whole, whole, half, half],
            out_specs=pl.BlockSpec((1, rows, cols), lambda slot, block, at: (slot, block, 0)),
        ),
        out_shape=jax.ShapeDtypeStruct((slots, 4 * rows, cols), own.dtype),
        compiler_params=pltpu.CompilerParams(vmem_limit_bytes=40 * 2**20),
        cost_estimate=pl.CostEstimate(
            flops=0, bytes_accessed=16 * slots * rows * cols, transcendentals=0
        ),
        name="assemble_weights",
    )(position, own, inner, outer, far_low, far_high)


def factor_kernel(gram_ref, factor_ref):
    def times(left, right):
        return lax.dot_general(
            left, right, (((1,), (0,)), ((), ())), precision=highest, preferred_element_type=f32
        )

    blocks = gram_ref.shape[0]
    row = lax.broadcasted_iota(jnp.int32, (MB, MB), 0)
    col = lax.broadcasted_iota(jnp.int32, (MB, MB), 1)
    eye = jnp.where(row == col, 1.0, 0.0).astype(f32)
    grams, factors = [], []
    for at in range(blocks):
        gram = gram_ref[at]
        trace = jnp.sum(jnp.sum(gram * eye, axis=1, keepdims=True), axis=0, keepdims=True)
        inverse = 1.0 / (jnp.sqrt(trace) + 1e-07)
        grams.append(gram * (inverse * inverse))
        factors.append(inverse)
    for step in range(NS):
        polys = [
            coef_one * eye + coef_two * gram + coef_three * times(gram, gram) for gram in grams
        ]
        if step == 0:
            factors = [poly * factor for poly, factor in zip(polys, factors)]
        else:
            factors = [times(factor, poly) for poly, factor in zip(polys, factors)]
        if step < NS - 1:
            grams = [times(gram, poly) for poly, gram in zip(polys, grams)]
            grams = [times(gram, poly) for poly, gram in zip(polys, grams)]
    for at in range(blocks):
        factor_ref[at] = factors[at]


def muon_factor(gram):
    count = gram.shape[0]
    step = next(size for size in (4, 2, 1) if count % size == 0)
    spec = pl.BlockSpec((step, MB, MB), lambda at: (at, 0, 0))
    return pl.pallas_call(
        factor_kernel,
        grid=(count // step,),
        in_specs=[spec],
        out_specs=spec,
        out_shape=jax.ShapeDtypeStruct(gram.shape, f32),
        compiler_params=pltpu.CompilerParams(vmem_limit_bytes=16 * 2**20),
        cost_estimate=pl.CostEstimate(
            flops=6 * 34 * count * MB**3, bytes_accessed=8 * count * MB**2, transcendentals=0
        ),
        name="muon_factor",
    )(gram)


def solution(mesh):
    n_dp, n_mp = mesh.shape["dp"], mesh.shape["mp"]

    def program(tokens, memory, mem_lengths, *rest):
        group_seqs = mem_lengths.shape[0] // n_dp
        team = n_mp // group_seqs
        paired = team == 2 and n_dp % 2 == 0
        row_count = n_dp // 2 if paired else n_dp
        row_axes = tuple(f"r{at}" for at in range(row_count.bit_length() - 1))
        pair_axes = ("c",) if paired else ()
        names = row_axes + pair_axes + ("s", "t")
        sizes = (2,) * (len(names) - 2) + (group_seqs, team)
        fine = Mesh(mesh.devices.reshape(sizes), names)
        row_spec, col_spec = row_axes + pair_axes, ("s", "t")
        tok_spec = P(names, None)
        mat_spec = P(None, row_spec, col_spec)
        body = functools.partial(on_device, row_axes, paired, group_seqs, team)
        return jax.shard_map(
            body,
            mesh=fine,
            in_specs=(tok_spec, tok_spec, P(row_spec), tok_spec)
            + (mat_spec,) * 4 + (P(),) * 3,
            out_specs=(tok_spec,) * 3 + (mat_spec,) * 4 + (P(),) * 4,
            check_vma=False,
        )(tokens, memory, mem_lengths, *rest)

    return program


def on_device(
    row_axes,
    paired,
    group_seqs,
    team,
    tokens,
    memory,
    mem_lengths,
    cotangent,
    attn_weights,
    ffn_weights,
    attn_momentum,
    ffn_momentum,
    norm_params,
    norm_first,
    norm_second,
):
    team_axis = "c" if paired else "t"
    col_axes = ("s", "t") if paired else ("s",)
    me = lax.axis_index(team_axis)
    row_total = 2 ** len(row_axes)
    col_total = group_seqs * (team if paired else 1)
    both_ways = [(0, 1), (1, 0)]

    def after(value, *others):
        return lax.optimization_barrier((value,) + others)[0]

    def place(value):
        if not paired:
            return value
        moved = lax.ppermute(value, ("c", "t"), [(1, 2), (2, 1)])
        return jnp.where(me == lax.axis_index("t"), value, moved)

    def team_gather(rows):
        if team == 2:
            other = lax.ppermute(rows, team_axis, both_ways)
            return jnp.concatenate([rows, other], axis=0)
        return lax.all_gather(rows, team_axis, axis=0, tiled=True)

    def team_scatter(product, rows):
        if team == 2:
            count = rows[0].shape[-2] // 2
            away = product(*[piece[..., count:, :] for piece in rows]).astype(bf16)
            arrived = lax.ppermute(away, team_axis, both_ways)
            return product(*[piece[..., :count, :] for piece in rows]) + arrived.astype(f32)
        return lax.psum_scatter(product(*rows), team_axis, scatter_dimension=0, tiled=True)

    def in_order(own, other, axis):
        first = jnp.where(me == 0, own, other)
        second = jnp.where(me == 0, other, own)
        return jnp.concatenate([first, second], axis=axis)

    def to_team(value):
        if not paired:
            return value
        cols = value.shape[2] // 2
        away = lax.dynamic_slice_in_dim(value, (1 - me) * cols, cols, 2)
        own = lax.dynamic_slice_in_dim(value, me * cols, cols, 2)
        return in_order(own, lax.ppermute(away, "c", both_ways), 1)

    def from_team(value):
        if not paired:
            return value
        rows = value.shape[1] // 2
        away = lax.dynamic_slice_in_dim(value, (1 - me) * rows, rows, 1)
        own = lax.dynamic_slice_in_dim(value, me * rows, rows, 1)
        return in_order(own, lax.ppermute(away, "c", both_ways), 2)

    def around(value, hop):
        pairs = [(at, (at + hop) % col_total) for at in range(col_total)]
        return lax.ppermute(value, col_axes, pairs)

    def gather_cols(shard):
        return jnp.concatenate([shard] + [around(shard, hop) for hop in range(1, col_total)], axis=2)

    def gather_rows(wide):
        slots, rows, cols = wide.shape
        if len(row_axes) != 2:
            full = lax.all_gather(wide, row_axes, axis=0, tiled=False)
            full = full.transpose(1, 0, 2, 3).reshape(slots, row_total * rows, cols)
            return full, full
        half = rows // 2
        by_outer = lax.ppermute(wide, row_axes[0], both_ways)
        by_inner = lax.ppermute(wide, row_axes[1], both_ways)
        far_low = lax.ppermute(by_outer[:, :half], row_axes[1], both_ways)
        far_high = lax.ppermute(by_inner[:, half:], row_axes[0], both_ways)
        position = lax.axis_index(row_axes).astype(jnp.int32)[None]
        full = assemble(position, wide, by_inner, by_outer, far_low, far_high)
        return full, far_high

    def split_features(rows, axis, other):
        pieces = 2 ** row_axes.index(axis)
        width = rows.shape[1] // (2 * pieces)
        here = lax.axis_index(axis)
        side = 1 - here if other else here
        cuts = [
            lax.dynamic_slice_in_dim(rows, (2 * piece + side) * width, width, 1)
            for piece in range(pieces)
        ]
        return cuts[0] if pieces == 1 else jnp.concatenate(cuts, axis=1)

    def grad_product(rows, grads):
        if grads.ndim == 2:
            grads = grads[None]
        return jnp.einsum("td,ktc->kdc", rows, grads, preferred_element_type=f32)

    def start_grad(rows, grads, axis):
        away = grad_product(split_features(rows, axis, True), grads).astype(bf16)
        return lax.ppermute(away, axis, both_ways)

    def finish_grad(arrived, rows, grads, order, *others):
        if others:
            arrived = after(arrived, *others)
        own = grad_product(split_features(rows, order[0], False), grads)
        piece = (own + arrived.astype(f32)).astype(bf16)
        left = [axis for axis in row_axes if axis != order[0]]
        slots, _, cols = piece.shape
        piece = piece.reshape((slots,) + (2,) * len(left) + (-1, cols))
        for axis in order[1:]:
            at = 1 + left.index(axis)
            here = lax.axis_index(axis)
            away = lax.dynamic_index_in_dim(piece, 1 - here, at, keepdims=False)
            own = lax.dynamic_index_in_dim(piece, here, at, keepdims=False)
            arrived = lax.ppermute(away, axis, both_ways)
            piece = (own.astype(f32) + arrived.astype(f32)).astype(bf16)
            left.remove(axis)
        return piece

    def scatter_cols(pieces, *others):
        if others:
            pieces = list(lax.optimization_barrier(tuple(pieces) + others)[: len(pieces)])
        width = pieces[0].shape[2] // col_total

        def part(hop):
            cut = [piece[:, :, hop * width : (hop + 1) * width] for piece in pieces]
            return jnp.concatenate(cut, axis=0)

        total = part(0).astype(f32)
        for hop in range(1, col_total):
            total = total + around(part(hop), col_total - hop).astype(f32)
        return total

    def muon(momentum, grad, beside):
        slots, rows, cols = momentum.shape
        fresh = 0.5 * momentum + grad
        blocks = fresh.reshape(slots, rows, cols // MB, MB)
        gram = jnp.einsum(
            "sdbi,sdbj->sbij", blocks, blocks, precision=highest, preferred_element_type=f32
        )
        extra = [] if beside is None else [beside]
        sums = jnp.concatenate([gram.reshape(-1, MB)] + extra, axis=0)
        for axis in row_axes:
            sums = sums + lax.ppermute(sums, axis, both_ways)
        count = gram.size // MB
        gram, beside = sums[:count].reshape(gram.shape), sums[count:]
        factor = muon_factor(gram.reshape(-1, MB, MB)).reshape(gram.shape)
        turned = jnp.einsum(
            "sdbi,sbij->sdbj", blocks, factor, precision=highest, preferred_element_type=f32
        )
        return fresh, turned.reshape(slots, rows, cols), beside

    def update(weights, momentum, grad, beside=None):
        fresh, turned, beside = muon(momentum, grad, beside)
        slots = fresh.shape[0]
        both = from_team(jnp.concatenate([fresh, turned], axis=0))
        return both[:slots], weights - step_scale * both[slots:], beside

    step_scale = muon_rate * (attn_weights.shape[1] * row_total * (2 if paired else 1) / MB) ** 0.5
    inner_axis, outer_axis = row_axes[-1], row_axes[0]
    down = row_axes[::-1]
    up = row_axes

    self_mine = to_team(attn_weights[:3].astype(bf16))
    own_tokens = place(tokens)
    self_wide = gather_cols(self_mine)
    own_tokens, rest_src = lax.optimization_barrier((own_tokens, attn_weights[3:]))
    token_rows = team_gather(own_tokens)
    w_qkv, last = gather_rows(self_wide)

    rest_wide = gather_cols(after(to_team(rest_src.astype(bf16)), self_wide))
    own_memory = place(memory)
    lengths = place(mem_lengths)
    length = lax.dynamic_slice_in_dim(lengths, lax.axis_index("s"), 1, 0)
    shift = me * own_tokens.shape[0] if paired else jnp.zeros((), jnp.int32)
    at = jnp.concatenate([length, shift.astype(jnp.int32)[None]])
    w_rest, last = gather_rows(after(rest_wide, last))
    ffn_wide = gather_cols(after(to_team(ffn_weights.astype(bf16)), rest_wide))
    u_both, _ = gather_rows(after(ffn_wide, last))
    u_in, u_out = u_both[0], u_both[1]
    w_so, w_cq = w_rest[0], w_rest[1]
    w_ckv, w_co = w_rest[2:4], w_rest[4]
    own_cotangent = place(after(cotangent, ffn_wide))

    def project(rows, weights):
        return jnp.einsum("td,kdc->ktc", rows, weights, preferred_element_type=f32).astype(bf16)

    def back(rows, weight):
        return jnp.einsum("tc,dc->td", rows, weight, preferred_element_type=f32)

    def back_pair(rows, weights):
        return back(rows[0], weights[0]) + back(rows[1], weights[1])

    def gain(index):
        return norm_params[0, index]

    def bias(index):
        return norm_params[1, index]

    qkv = project(token_rows, w_qkv)
    self_ctx, self_lse = attend_forward((qkv, 0), (qkv, 1), (qkv, 2), at, True)
    self_out = team_scatter(lambda rows: back(rows, w_so), [self_ctx])
    first_out, normed_one, inv_one = norm_forward(
        res_scale * own_tokens.astype(f32) + self_out, gain(0), bias(0)
    )
    first_rows = team_gather(first_out.astype(bf16))
    memory_rows = team_gather(own_memory)
    cross_kv = project(memory_rows, w_ckv)
    cross_q = project(first_rows, w_cq[None])
    cross_ctx, cross_lse = attend_forward((cross_q, 0), (cross_kv, 0), (cross_kv, 1), at, False)
    cross_out = team_scatter(lambda rows: back(rows, w_co), [cross_ctx])
    second, normed_two, inv_two = norm_forward(
        res_scale * first_out + cross_out, gain(1), bias(1)
    )
    second_rows = team_gather(second.astype(bf16))
    hidden = jnp.dot(second_rows, u_in, preferred_element_type=f32)
    active = gelu_exact(hidden).astype(bf16)
    ffn_out = team_scatter(lambda rows: back(rows, u_out), [active])
    mixed_out, normed_three, inv_three = norm_forward(
        res_scale * second + ffn_out, gain(2), bias(2)
    )

    grad_three, gain_three, bias_three = norm_backward(
        own_cotangent.astype(f32), normed_three, inv_three, gain(2)
    )
    grad_ffn_rows = team_gather(grad_three.astype(bf16))
    u_out_way = start_grad(grad_ffn_rows, active, inner_axis)
    grad_active = jnp.dot(grad_ffn_rows, u_out, preferred_element_type=f32)
    grad_hidden = (grad_active * gelu_slope(hidden)).astype(bf16)
    ffn_back = team_scatter(lambda rows: back(rows, u_in), [grad_hidden])
    u_in_way = start_grad(second_rows, grad_hidden, outer_axis)
    grad_second = res_scale * grad_three + ffn_back
    grad_two, gain_two, bias_two = norm_backward(grad_second, normed_two, inv_two, gain(1))
    grad_cross_rows = team_gather(grad_two.astype(bf16))
    grad_cross_ctx = jnp.dot(grad_cross_rows, w_co, preferred_element_type=f32).astype(bf16)
    grad_cq, grad_ckv = attend_backward(
        (cross_q, 0), (cross_kv, 0), (cross_kv, 1), at, cross_ctx, grad_cross_ctx,
        cross_lse, False,
    )
    first_back = team_scatter(lambda rows: back(rows, w_cq), [grad_cq])
    u_out_piece = finish_grad(u_out_way, grad_ffn_rows, active, down, grad_cq)
    u_in_piece = finish_grad(u_in_way, second_rows, grad_hidden, up, grad_cq)
    w7_way = start_grad(after(grad_cross_rows, grad_cq), cross_ctx, inner_axis)
    w4_way = start_grad(first_rows, grad_cq, inner_axis)
    w56_way = start_grad(memory_rows, grad_ckv, outer_axis)
    grad_first = res_scale * grad_two + first_back
    grad_one, gain_one, bias_one = norm_backward(grad_first, normed_one, inv_one, gain(0))
    grad_self_rows = team_gather(grad_one.astype(bf16))
    norm_part = jnp.stack(
        [jnp.stack([gain_one, gain_two, gain_three]), jnp.stack([bias_one, bias_two, bias_three])]
    )
    grad_self_ctx = jnp.dot(grad_self_rows, w_so, preferred_element_type=f32).astype(bf16)
    memory_grad = team_scatter(lambda rows: back_pair(rows, w_ckv), [grad_ckv])
    grad_sq, grad_skv = attend_backward(
        (qkv, 0), (qkv, 1), (qkv, 2), at, self_ctx, grad_self_ctx, self_lse, True
    )
    ffn_grad = scatter_cols([u_in_piece, u_out_piece])
    norm_part = after(norm_part, grad_sq)
    for axis in (("c",) if paired else ()) + ("s", "t"):
        if lax.axis_size(axis) == 2:
            norm_part = norm_part + lax.ppermute(norm_part, axis, both_ways)
        else:
            norm_part = lax.psum(norm_part, axis)
    w3_way = start_grad(grad_self_rows, self_ctx, inner_axis)
    w0_way = start_grad(token_rows, grad_sq, inner_axis)
    w12_way = start_grad(token_rows, grad_skv, outer_axis)
    w7_piece = finish_grad(w7_way, grad_cross_rows, cross_ctx, down, grad_sq)
    w4_piece = finish_grad(w4_way, first_rows, grad_cq, down, grad_sq)
    w56_piece = finish_grad(w56_way, memory_rows, grad_ckv, up, grad_sq)
    token_back = team_scatter(
        lambda q_rows, kv_rows: back(q_rows, w_qkv[0]) + back_pair(kv_rows, w_qkv[1:3]),
        [grad_sq, grad_skv],
    )
    input_grad = res_scale * grad_one + token_back
    w3_piece = finish_grad(w3_way, grad_self_rows, self_ctx, down)
    w0_piece = finish_grad(w0_way, token_rows, grad_sq, down)
    w12_piece = finish_grad(w12_way, token_rows, grad_skv, up)
    cross_grad = scatter_cols([w4_piece, w56_piece, w7_piece])
    self_grad = scatter_cols([w0_piece, w12_piece, w3_piece])

    attn_mom = to_team(attn_momentum)
    ffn_mom = to_team(ffn_momentum)
    ffn_momentum_new, ffn_weights_new, _ = update(ffn_weights, ffn_mom, ffn_grad)
    cross_momentum_new, cross_weights_new, _ = update(attn_weights[4:8], attn_mom[4:8], cross_grad)
    self_momentum_new, self_weights_new, norm_grad = update(
        attn_weights[0:4], attn_mom[0:4], self_grad, norm_part.reshape(-1, MB)
    )
    norm_grad = norm_grad.reshape(norm_params.shape)
    attn_momentum_new = jnp.concatenate([self_momentum_new, cross_momentum_new])
    attn_weights_new = jnp.concatenate([self_weights_new, cross_weights_new])

    norm_first_new = 0.9 * norm_first + 0.1 * norm_grad
    norm_second_new = 0.999 * norm_second + 0.001 * norm_grad * norm_grad
    step_size = (
        norm_first_new
        / (1.0 - 0.9**adam_count)
        / (jnp.sqrt(norm_second_new / (1.0 - 0.999**adam_count)) + 1e-08)
    )
    norm_params_new = norm_params - adam_rate * step_size
    return (
        place(mixed_out),
        place(input_grad),
        place(memory_grad),
        attn_weights_new,
        attn_momentum_new,
        ffn_weights_new,
        ffn_momentum_new,
        norm_grad,
        norm_params_new,
        norm_first_new,
        norm_second_new,
    )
```
